32 devices in a mesh: rep: 4 (over y, core), sp: 8 (over z, x).
Axes of the slice: x: 2, y: 2, z: 4, core: 2. Of those that a mesh axis runs over, the one named last changes fastest.
Arguments:
- queries: bfloat16 [8192, 8192], P(('rep', 'sp')), may hold values from -12 to 12
- keys: bfloat16 [8192, 1024], P(('rep', 'sp')), may hold values from -12 to 12
- values: bfloat16 [8192, 1024], P(('rep', 'sp')), may hold values from -6 to 6
- doc_lengths: int32 [4, 16], P('rep'), may hold values from 1 to 512, 2048 in all within a row
- dest_group: int32 [4, 64], replicated, may hold values from 0 to 3, as said below
- dest_slot: int32 [4, 64], replicated, may hold values from 0 to 7, as said below
Outputs:
- attended: bfloat16 [8192, 8192], P(('rep', 'sp'))
The draws below stay inside these ranges and needn't reach their ends.
Inputs may be any that keep to these rules, and one draw needn't show every extreme that they name: Piece j of sp index s of group g goes to the same sp index of group dest_group[g, s * 8 + j]; the 8 pieces of each device go to exactly half of the 4 groups, 4 to each. `dest_slot`: on every device of every group each of the 8 slots receives exactly one piece.
All inputs are finite; a program needn't handle non-finite values.
Results may differ from the reference program's by a relative error of at most 0.004.
Values may be sent and summed in bfloat16 or wider, within the bound.
A program may use at most 192 MiB of HBM per device.

```python
import math
import jax
import jax.numpy as jnp
import numpy as np
from jax import lax

QUERY_HEADS = 64
KEY_VALUE_HEADS = 8
HEAD_WIDTH = 128
DEVICE_PIECES = 8
TILE_ROWS = 512
NDOC = 16
PIECE_LENGTH = 32
STREAM = 2048
TOKEN_TOTAL = 8192
MOSTDOC = 512
N_REP = 4
N_SP = 8


def route_tables(key):
    folded = jax.random.fold_in(key, 71)
    key_sigma, key_source, key_target = jax.random.split(folded, 3)
    capacity = 2 * DEVICE_PIECES // N_REP
    sigma = jax.vmap(lambda inner: jax.random.permutation(inner, N_REP))(jax.random.split(key_sigma, N_SP))
    source_perm = jax.vmap(lambda inner: jax.random.permutation(inner, DEVICE_PIECES))(jax.random.split(key_source, N_REP * N_SP)).reshape(N_REP, N_SP, DEVICE_PIECES)
    target_perm = jax.vmap(lambda inner: jax.random.permutation(inner, DEVICE_PIECES))(jax.random.split(key_target, N_REP * N_SP)).reshape(N_REP, N_SP, DEVICE_PIECES)
    groups = jnp.arange(N_REP, dtype=jnp.int32)[:, None, None]
    shards = jnp.arange(N_SP, dtype=jnp.int32)[None, :, None]
    orders = jnp.arange(DEVICE_PIECES, dtype=jnp.int32)[None, None, :]
    target = sigma[shards, (groups + orders // capacity) % N_REP]
    slot_table = target_perm[target, shards, orders]
    inverse = jnp.argsort(source_perm, axis=2)
    group_out = jnp.take_along_axis(target, inverse, axis=2)
    slot_out = jnp.take_along_axis(slot_table, inverse, axis=2)
    return (group_out.reshape(N_REP, N_SP * DEVICE_PIECES).astype(jnp.int32), slot_out.reshape(N_REP, N_SP * DEVICE_PIECES).astype(jnp.int32))


def draw_dest_group(key, part):
    return route_tables(key)[0]


def draw_dest_slot(key, part):
    return route_tables(key)[1]


def query_key(key):
    folded = jax.random.fold_in(key, 29)
    key_query, random_key_seed = jax.random.split(folded, 2)
    query_row_data = jax.random.truncated_normal(key_query, -6.0, 6.0, (TOKEN_TOTAL, QUERY_HEADS * HEAD_WIDTH), jnp.float32)
    key_row_data = jax.random.truncated_normal(random_key_seed, -6.0, 6.0, (TOKEN_TOTAL, KEY_VALUE_HEADS * HEAD_WIDTH), jnp.float32)
    return (query_row_data, key_row_data)


def draw_queries(key, part):
    return query_key(key)[0].astype(jnp.bfloat16)


def draw_keys(key, part):
    return query_key(key)[1].astype(jnp.bfloat16)


def shard_levels(key, dims, cuts, smallest, largest):
    loudness, own = 1.0, jax.random.fold_in(key, 6)
    for axis_at, shards_of in cuts:
        draws = jnp.exp(jax.random.uniform(jax.random.fold_in(own, axis_at), (shards_of,), jnp.float32, smallest / len(cuts), largest / len(cuts)))
        loudness = loudness * jnp.repeat(draws, dims[axis_at] // shards_of).reshape([-1 if axis == axis_at else 1 for axis in range(len(dims))])
    return loudness


def profile(count, total, reach, skew):
    weights = [(1 << 20) // math.isqrt(standing ** skew) + 1 for standing in range(2, count + 1)]
    rest, given = total - reach - (count - 1), [1] * (count - 1)
    while rest > 0:
        candidates = [i for i in range(count - 1) if given[i] < reach]
        whole, left = sum([weights[i] for i in candidates]), rest
        for i in candidates:
            extra = min(reach - given[i], max(1, left * weights[i] // whole), rest)
            given[i] = given[i] + extra
            rest = rest - extra
    return np.array([reach] + given)


def ragged_sizes(key, count, total, bound, skew):
    if count == 2:
        one = jax.random.randint(key, (), max(1, total - bound), min(bound, total - 1) + 1)
        return jnp.stack([one, total - one])
    sizes = jnp.asarray(profile(count, total, bound, skew), jnp.int32)
    couples = (count - 1) // 2
    source_of, taker = sizes[1:1 + 2 * couples:2], sizes[2:2 + 2 * couples:2]
    slack = jnp.minimum(source_of - 1, bound - taker)
    passed = jax.random.randint(jax.random.fold_in(key, 1), (couples,), 0, 1 << 20) % (slack + 1)
    sizes = sizes.at[1:1 + 2 * couples:2].set(source_of - passed).at[2:2 + 2 * couples:2].set(taker + passed)
    return sizes[jax.random.permutation(jax.random.fold_in(key, 2), count)]


def bell_draw(key, dims, scale, most, cuts=(), kind=jnp.bfloat16):
    level = shard_levels(key, dims, cuts, -0.22, 0.18) if cuts else 1.0
    entries = jax.random.normal(key, dims, jnp.float32) * scale * level
    return jnp.minimum(jnp.maximum(entries, -most), most).astype(kind)


def setup_inputs(seed: int = 0) -> dict:
    arg_keys = jax.random.split(jax.random.key(seed), 7)
    return {
        "queries": draw_queries(jax.random.fold_in(arg_keys[6], 71), 0),
        "keys": draw_keys(jax.random.fold_in(arg_keys[6], 71), 0),
        "values": bell_draw(arg_keys[2], (TOKEN_TOTAL, KEY_VALUE_HEADS * HEAD_WIDTH), 1.0, 6.0, ((0, 32),)),
        "doc_lengths": jax.vmap(lambda own: ragged_sizes(own, NDOC, STREAM, MOSTDOC, 2))(jax.random.split(arg_keys[3], N_REP)).reshape((N_REP, NDOC)).astype(jnp.int32),
        "dest_group": draw_dest_group(jax.random.fold_in(arg_keys[6], 71), 0),
        "dest_slot": draw_dest_slot(jax.random.fold_in(arg_keys[6], 71), 0),
    }


MASKED = -1e+30

def doc_starts(positions, lengths):
    doc_ends = jnp.cumsum(lengths)
    return lax.optimization_barrier(jnp.sum(jnp.where(positions[:, None] >= doc_ends[None, :], lengths[None, :], 0), axis=1))

def place_pieces(row_data, dest_group, dest_slot):
    feature_width = row_data.shape[1]
    pieces = row_data.reshape(N_REP * N_SP * DEVICE_PIECES, PIECE_LENGTH, feature_width)
    shard_index = (jnp.arange(N_SP * DEVICE_PIECES, dtype=jnp.int32) // DEVICE_PIECES)[None, :]
    target = (dest_group * (N_SP * DEVICE_PIECES) + shard_index * DEVICE_PIECES + dest_slot).reshape(-1).astype(jnp.int32)
    placed = jnp.zeros_like(pieces).at[target].set(pieces)
    return placed.reshape(N_REP, STREAM, feature_width)

def group_attention(operands):
    grouped_queries, grouped_keys, grouped_values, lengths = operands
    positions = jnp.arange(STREAM, dtype=jnp.int32)
    starts = doc_starts(positions, lengths)
    heads_per_group = QUERY_HEADS // KEY_VALUE_HEADS
    score_scale = 1.0 / math.sqrt(HEAD_WIDTH)
    blocks = []
    for block_index in range(STREAM // TILE_ROWS):
        row_begin = block_index * TILE_ROWS
        row_stop = row_begin + TILE_ROWS
        allowed = (starts[row_begin:row_stop, None] == starts[None, :row_stop]) & (positions[row_begin:row_stop, None] >= positions[None, :row_stop])

        def one_head(head_ops, allowed=allowed):
            head_query, head_key, head_value = head_ops
            scores = jnp.einsum('qgd,kd->qgk', head_query.astype(jnp.float32), head_key.astype(jnp.float32)) * score_scale
            scores = jnp.where(allowed[:, None, :], scores, MASKED)
            row_peak = lax.optimization_barrier(jnp.max(scores, axis=2, keepdims=True))
            exponent = jnp.exp(scores - row_peak)
            row_total = lax.optimization_barrier(jnp.sum(exponent, axis=2))
            weights = exponent.astype(jnp.bfloat16)
            summed = jnp.einsum('qgk,kd->qgd', weights.astype(jnp.float32), head_value.astype(jnp.float32))
            return summed / row_total[:, :, None]
        query_block_rows = grouped_queries[row_begin:row_stop].reshape(TILE_ROWS, KEY_VALUE_HEADS, heads_per_group, HEAD_WIDTH).transpose(1, 0, 2, 3)
        key_block_rows = grouped_keys[:row_stop].reshape(row_stop, KEY_VALUE_HEADS, HEAD_WIDTH).transpose(1, 0, 2)
        value_block_rows = grouped_values[:row_stop].reshape(row_stop, KEY_VALUE_HEADS, HEAD_WIDTH).transpose(1, 0, 2)
        result = lax.map(one_head, (query_block_rows, key_block_rows, value_block_rows))
        blocks.append(result.transpose(1, 0, 2, 3).reshape(TILE_ROWS, QUERY_HEADS * HEAD_WIDTH))
    return jnp.concatenate(blocks, axis=0)

def reference(queries, keys, values, doc_lengths, dest_group, dest_slot):
    placed_query = place_pieces(queries, dest_group, dest_slot)
    placed_key = place_pieces(keys, dest_group, dest_slot)
    placed_value = place_pieces(values, dest_group, dest_slot)
    outputs = lax.map(group_attention, (placed_query, placed_key, placed_value, doc_lengths))
    return outputs.reshape(TOKEN_TOTAL, QUERY_HEADS * HEAD_WIDTH).astype(jnp.bfloat16)
```

```python
import functools
import math

import jax
import jax.numpy as jnp
from jax import lax
from jax.experimental import pallas as pl
from jax.experimental.pallas import tpu as pltpu
from jax.sharding import PartitionSpec as P

QUERY_HEADS = 64
KEY_VALUE_HEADS = 8
HEAD_WIDTH = 128
DEVICE_PIECES = 8
PIECE_LENGTH = 32
HEADS_PER_KV = QUERY_HEADS // KEY_VALUE_HEADS
CHUNK = HEADS_PER_KV * HEAD_WIDTH
CHUNKS = KEY_VALUE_HEADS
BLOCK = DEVICE_PIECES * PIECE_LENGTH
HALF_PIECES = 4
HALF_ROWS = HALF_PIECES * PIECE_LENGTH
DEPTH = 3

MASKED = -1e30
MESH = pl.DeviceIdType.MESH


def kernel(
    groups,
    shard_count,
    halo,
    lengths_ref,
    group_ref,
    slot_ref,
    q_hbm,
    k_hbm,
    v_hbm,
    o_hbm,
    *scratch,
):
    qbufs = scratch[:CHUNKS]
    (
        kbuf,
        vbuf,
        kp,
        vp,
        bias,
        qsel,
        obuf,
        sel,
        local_sem,
        y_send,
        y_recv,
        m_send,
        m_recv,
        f_send,
        f_recv,
        halo_send,
        halo_recv,
        out_sem,
    ) = scratch[CHUNKS:]
    rep = lax.axis_index("rep")
    shard = lax.axis_index("sp")
    chips = groups // 2
    core = lax.rem(rep, 2)
    chip = lax.div(rep, 2)
    mate = chip * 2 + (1 - core)
    window = halo * BLOCK + HALF_ROWS
    own_first = halo * BLOCK

    def peer(step):
        return lax.rem(chip + step, chips) * 2 + core

    def source(step):
        return lax.rem(chip + chips - step, chips) * 2 + core

    def mate_source(step):
        return lax.rem(chip + chips - step, chips) * 2 + (1 - core)

    items = CHUNKS + 2

    def original(item):
        if item == 0:
            return k_hbm
        if item == 1:
            return v_hbm
        return q_hbm.at[:, :, pl.ds((item - 2) * CHUNK, CHUNK)]

    def landing(item, group):
        buffer = (kbuf, vbuf, *qbufs)[item]
        return buffer.at[pl.ds(group * DEVICE_PIECES, DEVICE_PIECES)]

    def local_copy(item):
        return pltpu.make_async_copy(original(item), landing(item, rep), local_sem.at[item])

    def mate_copy(item, group):
        return pltpu.make_async_remote_copy(
            src_ref=original(item),
            dst_ref=landing(item, group),
            send_sem=m_send.at[item],
            recv_sem=m_recv.at[item],
            device_id={"rep": mate},
            device_id_type=MESH,
        )

    def peer_copy(item, step, group):
        return pltpu.make_async_remote_copy(
            src_ref=original(item),
            dst_ref=landing(item, group),
            send_sem=y_send.at[item, step - 1],
            recv_sem=y_recv.at[item, step - 1],
            device_id={"rep": peer(step)},
            device_id_type=MESH,
        )

    def forward_copy(item, step, group):
        return pltpu.make_async_remote_copy(
            src_ref=landing(item, group),
            dst_ref=landing(item, group),
            send_sem=f_send.at[item, step - 1],
            recv_sem=f_recv.at[item, step - 1],
            device_id={"rep": mate},
            device_id_type=MESH,
        )

    def start_out(item):
        for step in range(1, chips):
            peer_copy(item, step, rep).start()

    def start_near(item):
        mate_copy(item, rep).start()
        local_copy(item).start()

    def pass_on(item):
        for step in range(1, chips):
            peer_copy(item, step, source(step)).wait_recv()
            forward_copy(item, step, source(step)).start()

    def all_here(item):
        local_copy(item).wait()
        mate_copy(item, mate).wait_recv()
        for step in range(1, chips):
            forward_copy(item, step, mate_source(step)).wait_recv()

    def halo_copy(which, distance):
        placed = (kp, vp)[which]
        return pltpu.make_async_remote_copy(
            src_ref=placed.at[:, pl.ds(own_first, BLOCK), :],
            dst_ref=placed.at[:, pl.ds((halo - distance) * BLOCK, BLOCK), :],
            send_sem=halo_send.at[which, distance - 1],
            recv_sem=halo_recv.at[which, distance - 1],
            device_id={"sp": lax.rem(shard + distance, shard_count)},
            device_id_type=MESH,
        )

    barrier = pltpu.get_barrier_semaphore()
    pl.semaphore_signal(barrier, inc=1, device_id={"rep": mate}, device_id_type=MESH)
    for step in range(1, chips):
        pl.semaphore_signal(barrier, inc=1, device_id={"rep": peer(step)}, device_id_type=MESH)
    for distance in range(1, halo + 1):

        @pl.when(shard + distance < shard_count)
        def _():
            pl.semaphore_signal(
                barrier, inc=1, device_id={"sp": shard + distance}, device_id_type=MESH
            )

        @pl.when(shard >= distance)
        def _():
            pl.semaphore_signal(
                barrier, inc=1, device_id={"sp": shard - distance}, device_id_type=MESH
            )

    before = jnp.minimum(shard, halo)
    after = jnp.minimum(shard_count - 1 - shard, halo)
    pl.semaphore_wait(barrier, chips + before + after)

    for item in range(2):
        start_out(item)
    for item in range(2):
        start_near(item)
    for item in range(2, 2 + DEPTH):
        start_out(item)
        start_near(item)

    def find_slot(slot, carry):
        found = jnp.int32(0)
        for group in range(groups):
            for piece in range(DEVICE_PIECES):
                column = shard * DEVICE_PIECES + piece
                hit = (group_ref[group, column] == rep) & (slot_ref[group, column] == slot)
                found = jnp.where(hit, group * DEVICE_PIECES + piece, found)
        sel[slot] = found
        return carry

    lax.fori_loop(0, DEVICE_PIECES, find_slot, 0)

    def first_token(positions):
        end = jnp.int32(0)
        first = jnp.zeros_like(positions)
        for document in range(lengths_ref.shape[1]):
            length = lengths_ref[0, document]
            end = end + length
            first = first + jnp.where(positions >= end, length, 0)
        return first

    for half in range(2):
        key_begin = (shard - halo) * BLOCK + half * HALF_ROWS
        key_positions = key_begin + lax.broadcasted_iota(jnp.int32, (1, window), 1)
        key_first = jnp.where(key_positions >= 0, first_token(key_positions), -1)
        query_begin = shard * BLOCK + half * HALF_ROWS
        query_positions = query_begin + lax.broadcasted_iota(jnp.int32, (HALF_ROWS, 1), 0)
        query_first = first_token(query_positions)
        allowed = (query_first == key_first) & (query_positions >= key_positions)
        bias[pl.ds(half * HALF_ROWS, HALF_ROWS), :] = jnp.where(allowed, 0.0, MASKED)

    for distance in range(1, halo + 1):

        @pl.when(shard < distance)
        def _():
            empty = jnp.zeros((KEY_VALUE_HEADS, BLOCK, HEAD_WIDTH), jnp.bfloat16)
            kp[:, pl.ds((halo - distance) * BLOCK, BLOCK), :] = empty
            vp[:, pl.ds((halo - distance) * BLOCK, BLOCK), :] = empty

    for item in range(2):
        pass_on(item)
    for item in range(2):
        all_here(item)
        arrived, placed = (kbuf, vbuf)[item], (kp, vp)[item]
        for slot in range(DEVICE_PIECES):
            piece = arrived[sel[slot]]
            for head in range(KEY_VALUE_HEADS):
                placed[head, pl.ds(own_first + slot * PIECE_LENGTH, PIECE_LENGTH), :] = piece[
                    :, head * HEAD_WIDTH : (head + 1) * HEAD_WIDTH
                ]
        for distance in range(1, halo + 1):

            @pl.when(shard + distance < shard_count)
            def _():
                halo_copy(item, distance).start()

    factor = math.log2(math.e) / math.sqrt(HEAD_WIDTH)

    def out_copy(head):
        return pltpu.make_async_copy(
            obuf.at[lax.rem(head, 2)],
            o_hbm.at[:, pl.ds(pl.multiple_of(head * CHUNK, CHUNK), CHUNK)],
            out_sem.at[lax.rem(head, 2)],
        )

    def attend(head):
        buffer = lax.rem(head, 2)

        def one_piece(slot, carry):
            half = lax.div(slot, HALF_PIECES)
            keys_at = pl.ds(pl.multiple_of(half * HALF_ROWS, HALF_ROWS), window)
            rows_at = pl.ds(pl.multiple_of(slot * PIECE_LENGTH, PIECE_LENGTH), PIECE_LENGTH)
            piece = qsel[slot]
            query = jnp.concatenate(
                [piece[:, i * HEAD_WIDTH : (i + 1) * HEAD_WIDTH] for i in range(HEADS_PER_KV)],
                axis=0,
            )
            scores = lax.dot_general(
                query,
                kp[head, keys_at, :],
                (((1,), (1,)), ((), ())),
                preferred_element_type=jnp.float32,
            )
            scores = scores.reshape(HEADS_PER_KV, PIECE_LENGTH, window) * factor
            scores = (scores + bias[rows_at, :][None]).reshape(BLOCK, window)
            peak = jnp.max(scores, axis=1, keepdims=True)
            exponent = jnp.exp2(scores - peak)
            total = jnp.sum(exponent, axis=1, keepdims=True)
            summed = jnp.dot(
                exponent.astype(jnp.bfloat16),
                vp[head, keys_at, :],
                preferred_element_type=jnp.float32,
            )
            result = (summed / total).astype(jnp.bfloat16)
            for i in range(HEADS_PER_KV):
                obuf[buffer, rows_at, i * HEAD_WIDTH : (i + 1) * HEAD_WIDTH] = result[
                    i * PIECE_LENGTH : (i + 1) * PIECE_LENGTH
                ]
            return carry

        lax.fori_loop(0, DEVICE_PIECES, one_piece, 0)

    def turn(count, carry):
        for chunk in range(CHUNKS):

            @pl.when(count == chunk)
            def _():
                pass_on(2 + chunk)
                if chunk + DEPTH < CHUNKS:
                    for step in range(1, chips):
                        peer_copy(2 + chunk, step, rep).wait_send()
                    start_out(2 + chunk + DEPTH)
                    start_near(2 + chunk + DEPTH)

        @pl.when(count == 1)
        def _():
            for distance in range(1, halo + 1):

                @pl.when(shard >= distance)
                def _():
                    for which in range(2):
                        halo_copy(which, distance).wait_recv()

        for chunk in range(CHUNKS):

            @pl.when(count == chunk + 1)
            def _():
                all_here(2 + chunk)
                for slot in range(DEVICE_PIECES):
                    qsel[slot] = qbufs[chunk][sel[slot]]

        @pl.when(count >= 1)
        def _():
            head = count - 1

            @pl.when(count >= 3)
            def _():
                out_copy(head - 2).wait()

            attend(head)
            out_copy(head).start()

        return carry

    lax.fori_loop(0, CHUNKS + 1, turn, 0)

    for head in range(CHUNKS - 2, CHUNKS):
        out_copy(head).wait()
    for item in range(items):
        mate_copy(item, rep).wait_send()
        for step in range(1, chips):
            if item < 2 or item - 2 + DEPTH >= CHUNKS:
                peer_copy(item, step, rep).wait_send()
            forward_copy(item, step, source(step)).wait_send()
    for distance in range(1, halo + 1):

        @pl.when(shard + distance < shard_count)
        def _():
            for which in range(2):
                halo_copy(which, distance).wait_send()


def shards(queries, keys, values, doc_lengths, dest_group, dest_slot):
    groups = lax.axis_size("rep")
    shard_count = lax.axis_size("sp")
    chips = groups // 2
    halo = shard_count // 4
    pieces = groups * DEVICE_PIECES
    items = CHUNKS + 2
    key_rows = (halo + 1) * BLOCK
    window = halo * BLOCK + HALF_ROWS
    wide = KEY_VALUE_HEADS * HEAD_WIDTH
    smem = pl.BlockSpec(memory_space=pltpu.SMEM)
    hbm = pl.BlockSpec(memory_space=pl.ANY)
    dma = pltpu.SemaphoreType.DMA
    scratch = [pltpu.VMEM((pieces, PIECE_LENGTH, CHUNK), jnp.bfloat16) for _ in range(CHUNKS)]
    scratch += [
        pltpu.VMEM((pieces, PIECE_LENGTH, wide), jnp.bfloat16),
        pltpu.VMEM((pieces, PIECE_LENGTH, wide), jnp.bfloat16),
        pltpu.VMEM((KEY_VALUE_HEADS, key_rows, HEAD_WIDTH), jnp.bfloat16),
        pltpu.VMEM((KEY_VALUE_HEADS, key_rows, HEAD_WIDTH), jnp.bfloat16),
        pltpu.VMEM((BLOCK, window), jnp.float32),
        pltpu.VMEM((DEVICE_PIECES, PIECE_LENGTH, CHUNK), jnp.bfloat16),
        pltpu.VMEM((2, BLOCK, CHUNK), jnp.bfloat16),
        pltpu.SMEM((DEVICE_PIECES,), jnp.int32),
        dma((items,)),
        dma((items, chips - 1)),
        dma((items, chips - 1)),
        dma((items,)),
        dma((items,)),
        dma((items, chips - 1)),
        dma((items, chips - 1)),
        dma((2, halo)),
        dma((2, halo)),
        dma((2,)),
    ]
    work = QUERY_HEADS * BLOCK * window
    return pl.pallas_call(
        functools.partial(kernel, groups, shard_count, halo),
        out_shape=jax.ShapeDtypeStruct(queries.shape, jnp.bfloat16),
        in_specs=[smem, smem, smem, hbm, hbm, hbm],
        out_specs=hbm,
        scratch_shapes=scratch,
        cost_estimate=pl.CostEstimate(
            flops=4 * work * HEAD_WIDTH,
            bytes_accessed=4 * queries.size + 4 * keys.size,
            transcendentals=work,
        ),
        compiler_params=pltpu.CompilerParams(
            collective_id=0, has_side_effects=True, vmem_limit_bytes=56 * 1024 * 1024
        ),
    )(
        doc_lengths,
        dest_group,
        dest_slot,
        queries.reshape(DEVICE_PIECES, PIECE_LENGTH, QUERY_HEADS * HEAD_WIDTH),
        keys.reshape(DEVICE_PIECES, PIECE_LENGTH, wide),
        values.reshape(DEVICE_PIECES, PIECE_LENGTH, wide),
    )


def solution(mesh):
    return jax.shard_map(
        shards,
        mesh=mesh,
        in_specs=(
            P(("rep", "sp"), None),
            P(("rep", "sp"), None),
            P(("rep", "sp"), None),
            P("rep", None),
            P(),
            P(),
        ),
        out_specs=P(("rep", "sp"), None),
        check_vma=False,
    )
```

```python
import functools
import math

import jax
import jax.numpy as jnp
from jax import lax
from jax.experimental import pallas as pl
from jax.experimental.pallas import tpu as pltpu
from jax.sharding import PartitionSpec as P

QUERY_HEADS = 64
KEY_VALUE_HEADS = 8
HEAD_WIDTH = 128
DEVICE_PIECES = 8
PIECE_LENGTH = 32
HEADS_PER_KV = QUERY_HEADS // KEY_VALUE_HEADS
CHUNK = HEADS_PER_KV * HEAD_WIDTH
CHUNKS = KEY_VALUE_HEADS
BLOCK = DEVICE_PIECES * PIECE_LENGTH
HALF_PIECES = 4
HALF_ROWS = HALF_PIECES * PIECE_LENGTH
CAPACITY = 6
DEPTH = 3

MASKED = -1e30
MESH = pl.DeviceIdType.MESH


def kernel(
    groups,
    shard_count,
    halo,
    slim,
    lengths_ref,
    group_ref,
    slot_ref,
    q_hbm,
    k_hbm,
    v_hbm,
    o_hbm,
    *scratch,
):
    items = CHUNKS + 2
    buffers = scratch[:items]
    far = scratch[items : 2 * items]
    stage = scratch[2 * items : 3 * items]
    (
        kp,
        vp,
        bias,
        qsel,
        obuf,
        sel,
        far_sel,
        from_far,
        send_sel,
        local_sem,
        y_send,
        y_recv,
        m_send,
        m_recv,
        f_send,
        f_recv,
        halo_send,
        halo_recv,
        out_sem,
    ) = scratch[3 * items if slim else items :]
    rep = lax.axis_index("rep")
    shard = lax.axis_index("sp")
    chips = groups // 2
    core = lax.rem(rep, 2)
    chip = lax.div(rep, 2)
    mate = chip * 2 + (1 - core)
    window = halo * BLOCK + HALF_ROWS
    own_first = halo * BLOCK

    def peer(step):
        return lax.rem(chip + step, chips) * 2 + core

    def source(step):
        return lax.rem(chip + chips - step, chips) * 2 + core

    def mate_source(step):
        return lax.rem(chip + chips - step, chips) * 2 + (1 - core)


    def original(item):
        if item == 0:
            return k_hbm
        if item == 1:
            return v_hbm
        return q_hbm.at[:, :, pl.ds((item - 2) * CHUNK, CHUNK)]

    def landing(item, group):
        place = lax.rem(group, 2) if slim else group
        return buffers[item].at[pl.ds(place * DEVICE_PIECES, DEVICE_PIECES)]

    def crossing(item, group):
        if slim:
            return far[item].at[pl.ds(lax.rem(group, 2) * CAPACITY, CAPACITY)]
        return landing(item, group)

    def local_copy(item):
        return pltpu.make_async_copy(original(item), landing(item, rep), local_sem.at[item])

    def mate_copy(item, group):
        return pltpu.make_async_remote_copy(
            src_ref=original(item),
            dst_ref=landing(item, group),
            send_sem=m_send.at[item],
            recv_sem=m_recv.at[item],
            device_id={"rep": mate},
            device_id_type=MESH,
        )

    def peer_copy(item, step, group):
        return pltpu.make_async_remote_copy(
            src_ref=stage[item] if slim else original(item),
            dst_ref=crossing(item, group),
            send_sem=y_send.at[item, step - 1],
            recv_sem=y_recv.at[item, step - 1],
            device_id={"rep": peer(step)},
            device_id_type=MESH,
        )

    def forward_copy(item, step, group):
        return pltpu.make_async_remote_copy(
            src_ref=crossing(item, group),
            dst_ref=crossing(item, group),
            send_sem=f_send.at[item, step - 1],
            recv_sem=f_recv.at[item, step - 1],
            device_id={"rep": mate},
            device_id_type=MESH,
        )

    def near_here(item):
        local_copy(item).wait()
        mate_copy(item, mate).wait_recv()

    def start_out(item):
        if slim:
            near_here(item)
            for place in range(CAPACITY):
                stage[item][place] = buffers[item][send_sel[place]]
        for step in range(1, chips):
            peer_copy(item, step, rep).start()

    def start_near(item):
        mate_copy(item, rep).start()
        local_copy(item).start()

    def pass_on(item):
        for step in range(1, chips):
            peer_copy(item, step, source(step)).wait_recv()
            forward_copy(item, step, source(step)).start()

    def all_here(item):
        if not slim:
            near_here(item)
        for step in range(1, chips):
            forward_copy(item, step, mate_source(step)).wait_recv()

    def pick(item, slot):
        piece = buffers[item][sel[slot]]
        if slim:
            piece = jnp.where(from_far[slot] == 1, far[item][far_sel[slot]], piece)
        return piece

    def halo_copy(which, distance):
        placed = (kp, vp)[which]
        return pltpu.make_async_remote_copy(
            src_ref=placed.at[:, pl.ds(own_first, BLOCK), :],
            dst_ref=placed.at[:, pl.ds((halo - distance) * BLOCK, BLOCK), :],
            send_sem=halo_send.at[which, distance - 1],
            recv_sem=halo_recv.at[which, distance - 1],
            device_id={"sp": lax.rem(shard + distance, shard_count)},
            device_id_type=MESH,
        )

    barrier = pltpu.get_barrier_semaphore()
    pl.semaphore_signal(barrier, inc=1, device_id={"rep": mate}, device_id_type=MESH)
    for step in range(1, chips):
        pl.semaphore_signal(barrier, inc=1, device_id={"rep": peer(step)}, device_id_type=MESH)
    for distance in range(1, halo + 1):

        @pl.when(shard + distance < shard_count)
        def _():
            pl.semaphore_signal(
                barrier, inc=1, device_id={"sp": shard + distance}, device_id_type=MESH
            )

        @pl.when(shard >= distance)
        def _():
            pl.semaphore_signal(
                barrier, inc=1, device_id={"sp": shard - distance}, device_id_type=MESH
            )

    before = jnp.minimum(shard, halo)
    after = jnp.minimum(shard_count - 1 - shard, halo)
    pl.semaphore_wait(barrier, chips + before + after)

    if slim:
        for item in range(2):
            start_near(item)
    else:
        for item in range(2):
            start_out(item)
        for item in range(2):
            start_near(item)
        for item in range(2, 2 + DEPTH):
            start_out(item)
            start_near(item)

    def table_at(of_chip, number):
        group = of_chip * 2 + number // DEVICE_PIECES
        return group, shard * DEVICE_PIECES + number % DEVICE_PIECES

    def find_slot(slot, carry):
        found = jnp.int32(0)
        for number in range((2 if slim else groups) * DEVICE_PIECES):
            at = table_at(chip if slim else 0, number)
            hit = (group_ref[at] == rep) & (slot_ref[at] == slot)
            found = jnp.where(hit, number, found)
        sel[slot] = found
        if slim:
            far_found, is_far, rank = jnp.int32(0), jnp.int32(0), jnp.int32(0)
            for number in range(2 * DEVICE_PIECES):
                at = table_at(1 - chip, number)
                group = group_ref[at]
                hit = (group == rep) & (slot_ref[at] == slot)
                far_found = jnp.where(hit, rank, far_found)
                is_far = jnp.where(hit, 1, is_far)
                rank = rank + jnp.where((group >= 2) == (chip == 1), 1, 0)
            far_sel[slot] = jnp.minimum(far_found, 2 * CAPACITY - 1)
            from_far[slot] = is_far
        return carry

    def find_sent(place, carry):
        found, rank = jnp.int32(0), jnp.int32(0)
        for number in range(2 * DEVICE_PIECES):
            leaves = (group_ref[table_at(chip, number)] >= 2) == (chip == 0)
            found = jnp.where(leaves & (rank == core * CAPACITY + place), number, found)
            rank = rank + jnp.where(leaves, 1, 0)
        send_sel[place] = found
        return carry

    if slim:
        lax.fori_loop(0, CAPACITY, find_sent, 0)
        for item in range(2):
            start_out(item)
        for item in range(2, 3 + DEPTH):
            start_near(item)
        for item in range(2, 2 + DEPTH):
            start_out(item)
    lax.fori_loop(0, DEVICE_PIECES, find_slot, 0)

    def first_token(positions):
        end = jnp.int32(0)
        first = jnp.zeros_like(positions)
        for document in range(lengths_ref.shape[1]):
            length = lengths_ref[0, document]
            end = end + length
            first = first + jnp.where(positions >= end, length, 0)
        return first

    for half in range(2):
        key_begin = (shard - halo) * BLOCK + half * HALF_ROWS
        key_positions = key_begin + lax.broadcasted_iota(jnp.int32, (1, window), 1)
        key_first = jnp.where(key_positions >= 0, first_token(key_positions), -1)
        query_begin = shard * BLOCK + half * HALF_ROWS
        query_positions = query_begin + lax.broadcasted_iota(jnp.int32, (HALF_ROWS, 1), 0)
        query_first = first_token(query_positions)
        allowed = (query_first == key_first) & (query_positions >= key_positions)
        bias[pl.ds(half * HALF_ROWS, HALF_ROWS), :] = jnp.where(allowed, 0.0, MASKED)

    for distance in range(1, halo + 1):

        @pl.when(shard < distance)
        def _():
            empty = jnp.zeros((KEY_VALUE_HEADS, BLOCK, HEAD_WIDTH), jnp.bfloat16)
            kp[:, pl.ds((halo - distance) * BLOCK, BLOCK), :] = empty
            vp[:, pl.ds((halo - distance) * BLOCK, BLOCK), :] = empty

    for item in range(2):
        pass_on(item)
    for item in range(2):
        all_here(item)
        placed = (kp, vp)[item]
        for slot in range(DEVICE_PIECES):
            piece = pick(item, slot)
            for head in range(KEY_VALUE_HEADS):
                placed[head, pl.ds(own_first + slot * PIECE_LENGTH, PIECE_LENGTH), :] = piece[
                    :, head * HEAD_WIDTH : (head + 1) * HEAD_WIDTH
                ]
        for distance in range(1, halo + 1):

            @pl.when(shard + distance < shard_count)
            def _():
                halo_copy(item, distance).start()

    factor = math.log2(math.e) / math.sqrt(HEAD_WIDTH)

    def out_copy(head):
        return pltpu.make_async_copy(
            obuf.at[lax.rem(head, 2)],
            o_hbm.at[:, pl.ds(pl.multiple_of(head * CHUNK, CHUNK), CHUNK)],
            out_sem.at[lax.rem(head, 2)],
        )

    def attend(head):
        buffer = lax.rem(head, 2)

        def one_piece(slot, carry):
            half = lax.div(slot, HALF_PIECES)
            keys_at = pl.ds(pl.multiple_of(half * HALF_ROWS, HALF_ROWS), window)
            rows_at = pl.ds(pl.multiple_of(slot * PIECE_LENGTH, PIECE_LENGTH), PIECE_LENGTH)
            piece = qsel[slot]
            query = jnp.concatenate(
                [piece[:, i * HEAD_WIDTH : (i + 1) * HEAD_WIDTH] for i in range(HEADS_PER_KV)],
                axis=0,
            )
            scores = lax.dot_general(
                query,
                kp[head, keys_at, :],
                (((1,), (1,)), ((), ())),
                preferred_element_type=jnp.float32,
            )
            scores = scores.reshape(HEADS_PER_KV, PIECE_LENGTH, window) * factor
            scores = (scores + bias[rows_at, :][None]).reshape(BLOCK, window)
            peak = jnp.max(scores, axis=1, keepdims=True)
            exponent = jnp.exp2(scores - peak)
            total = jnp.sum(exponent, axis=1, keepdims=True)
            summed = jnp.dot(
                exponent.astype(jnp.bfloat16),
                vp[head, keys_at, :],
                preferred_element_type=jnp.float32,
            )
            result = (summed / total).astype(jnp.bfloat16)
            for i in range(HEADS_PER_KV):
                obuf[buffer, rows_at, i * HEAD_WIDTH : (i + 1) * HEAD_WIDTH] = result[
                    i * PIECE_LENGTH : (i + 1) * PIECE_LENGTH
                ]
            return carry

        lax.fori_loop(0, DEVICE_PIECES, one_piece, 0)

    def turn(count, carry):
        for chunk in range(CHUNKS):

            @pl.when(count == chunk)
            def _():
                pass_on(2 + chunk)
                if chunk + DEPTH < CHUNKS:
                    for step in range(1, chips):
                        peer_copy(2 + chunk, step, rep).wait_send()
                    start_out(2 + chunk + DEPTH)
                    ahead = chunk + DEPTH + (1 if slim else 0)
                    if ahead < CHUNKS:
                        start_near(2 + ahead)

        @pl.when(count == 1)
        def _():
            for distance in range(1, halo + 1):

                @pl.when(shard >= distance)
                def _():
                    for which in range(2):
                        halo_copy(which, distance).wait_recv()

        for chunk in range(CHUNKS):

            @pl.when(count == chunk + 1)
            def _():
                all_here(2 + chunk)
                for slot in range(DEVICE_PIECES):
                    qsel[slot] = pick(2 + chunk, slot)

        @pl.when(count >= 1)
        def _():
            head = count - 1

            @pl.when(count >= 3)
            def _():
                out_copy(head - 2).wait()

            attend(head)
            out_copy(head).start()

        return carry

    lax.fori_loop(0, CHUNKS + 1, turn, 0)

    for head in range(CHUNKS - 2, CHUNKS):
        out_copy(head).wait()
    for item in range(items):
        mate_copy(item, rep).wait_send()
        for step in range(1, chips):
            if item < 2 or item - 2 + DEPTH >= CHUNKS:
                peer_copy(item, step, rep).wait_send()
            forward_copy(item, step, source(step)).wait_send()
    for distance in range(1, halo + 1):

        @pl.when(shard + distance < shard_count)
        def _():
            for which in range(2):
                halo_copy(which, distance).wait_send()


def gathered_attention(slim, groups, shard_count, operands):
    queries, keys, values, doc_lengths, dest_group, dest_slot = operands
    chips = groups // 2
    halo = shard_count // 4
    pieces = (2 if slim else groups) * DEVICE_PIECES
    items = CHUNKS + 2
    key_rows = (halo + 1) * BLOCK
    window = halo * BLOCK + HALF_ROWS
    wide = KEY_VALUE_HEADS * HEAD_WIDTH
    smem = pl.BlockSpec(memory_space=pltpu.SMEM)
    hbm = pl.BlockSpec(memory_space=pl.ANY)
    dma = pltpu.SemaphoreType.DMA
    widths = [wide] * 2 + [CHUNK] * CHUNKS
    scratch = []
    for count in (pieces, 2 * CAPACITY, CAPACITY) if slim else (pieces,):
        scratch += [pltpu.VMEM((count, PIECE_LENGTH, width), jnp.bfloat16) for width in widths]
    scratch += [
        pltpu.VMEM((KEY_VALUE_HEADS, key_rows, HEAD_WIDTH), jnp.bfloat16),
        pltpu.VMEM((KEY_VALUE_HEADS, key_rows, HEAD_WIDTH), jnp.bfloat16),
        pltpu.VMEM((BLOCK, window), jnp.float32),
        pltpu.VMEM((DEVICE_PIECES, PIECE_LENGTH, CHUNK), jnp.bfloat16),
        pltpu.VMEM((2, BLOCK, CHUNK), jnp.bfloat16),
        pltpu.SMEM((DEVICE_PIECES,), jnp.int32),
        pltpu.SMEM((DEVICE_PIECES,), jnp.int32),
        pltpu.SMEM((DEVICE_PIECES,), jnp.int32),
        pltpu.SMEM((CAPACITY,), jnp.int32),
        dma((items,)),
        dma((items, chips - 1)),
        dma((items, chips - 1)),
        dma((items,)),
        dma((items,)),
        dma((items, chips - 1)),
        dma((items, chips - 1)),
        dma((2, halo)),
        dma((2, halo)),
        dma((2,)),
    ]
    work = QUERY_HEADS * BLOCK * window
    return pl.pallas_call(
        functools.partial(kernel, groups, shard_count, halo, slim),
        out_shape=jax.ShapeDtypeStruct(queries.shape, jnp.bfloat16),
        in_specs=[smem, smem, smem, hbm, hbm, hbm],
        out_specs=hbm,
        scratch_shapes=scratch,
        cost_estimate=pl.CostEstimate(
            flops=4 * work * HEAD_WIDTH,
            bytes_accessed=4 * queries.size + 4 * keys.size,
            transcendentals=work,
        ),
        compiler_params=pltpu.CompilerParams(
            collective_id=1 if slim else 0, has_side_effects=True, vmem_limit_bytes=56 * 1024 * 1024
        ),
    )(
        doc_lengths,
        dest_group,
        dest_slot,
        queries.reshape(DEVICE_PIECES, PIECE_LENGTH, QUERY_HEADS * HEAD_WIDTH),
        keys.reshape(DEVICE_PIECES, PIECE_LENGTH, wide),
        values.reshape(DEVICE_PIECES, PIECE_LENGTH, wide),
    )


def shards(*operands):
    groups = lax.axis_size("rep")
    shard_count = lax.axis_size("sp")
    whole = functools.partial(gathered_attention, False, groups, shard_count)
    if groups != 4:
        return whole(operands)
    target_chip = operands[4].reshape(2, 2, shard_count, DEVICE_PIECES) // 2
    leaves = target_chip != jnp.arange(2)[:, None, None, None]
    fits = jnp.all(jnp.sum(leaves, axis=(1, 3)) <= 2 * CAPACITY)
    slim = functools.partial(gathered_attention, True, groups, shard_count)
    return lax.cond(fits, slim, whole, operands)


def solution(mesh):
    return jax.shard_map(
        shards,
        mesh=mesh,
        in_specs=(
            P(("rep", "sp"), None),
            P(("rep", "sp"), None),
            P(("rep", "sp"), None),
            P("rep", None),
            P(),
            P(),
        ),
        out_specs=P(("rep", "sp"), None),
        check_vma=False,
    )
```

```python
import functools
import math

import jax
import jax.numpy as jnp
from jax import lax
from jax.experimental import pallas as pl
from jax.experimental.pallas import tpu as pltpu
from jax.sharding import PartitionSpec as P

QUERY_HEADS = 64
KEY_VALUE_HEADS = 8
HEAD_WIDTH = 128
DEVICE_PIECES = 8
PIECE_LENGTH = 32
HEADS_PER_KV = QUERY_HEADS // KEY_VALUE_HEADS
CHUNK = HEADS_PER_KV * HEAD_WIDTH
CHUNKS = KEY_VALUE_HEADS
BLOCK = DEVICE_PIECES * PIECE_LENGTH
HALF_PIECES = 4
HALF_ROWS = HALF_PIECES * PIECE_LENGTH
PARTS = 4
PART_HEADS = KEY_VALUE_HEADS // PARTS
CAPACITY = 6
DEPTH = 3

MASKED = -1e30
MESH = pl.DeviceIdType.MESH


def kernel(
    groups,
    shard_count,
    halo,
    slim,
    lengths_ref,
    group_ref,
    slot_ref,
    q_hbm,
    k_hbm,
    v_hbm,
    o_hbm,
    *scratch,
):
    items = CHUNKS + 2
    buffers = scratch[:items]
    far = scratch[items : 2 * items]
    stage = scratch[2 * items : 3 * items]
    (
        kp,
        vp,
        bias,
        qsel,
        obuf,
        sel,
        far_sel,
        from_far,
        send_sel,
        local_sem,
        y_send,
        y_recv,
        m_send,
        m_recv,
        f_send,
        f_recv,
        halo_send,
        halo_recv,
        out_sem,
    ) = scratch[3 * items if slim else items :]
    rep = lax.axis_index("rep")
    shard = lax.axis_index("sp")
    chips = groups // 2
    core = lax.rem(rep, 2)
    chip = lax.div(rep, 2)
    mate = chip * 2 + (1 - core)
    window = halo * BLOCK + HALF_ROWS
    own_first = halo * BLOCK

    def peer(step):
        return lax.rem(chip + step, chips) * 2 + core

    def source(step):
        return lax.rem(chip + chips - step, chips) * 2 + core

    def mate_source(step):
        return lax.rem(chip + chips - step, chips) * 2 + (1 - core)


    def original(item):
        if item == 0:
            return k_hbm
        if item == 1:
            return v_hbm
        return q_hbm.at[:, :, pl.ds((item - 2) * CHUNK, CHUNK)]

    def landing(item, group):
        place = lax.rem(group, 2) if slim else group
        return buffers[item].at[pl.ds(place * DEVICE_PIECES, DEVICE_PIECES)]

    def crossing(item, group):
        if slim:
            return far[item].at[pl.ds(lax.rem(group, 2) * CAPACITY, CAPACITY)]
        return landing(item, group)

    def local_copy(item):
        return pltpu.make_async_copy(original(item), landing(item, rep), local_sem.at[item])

    def mate_copy(item, group):
        return pltpu.make_async_remote_copy(
            src_ref=original(item),
            dst_ref=landing(item, group),
            send_sem=m_send.at[item],
            recv_sem=m_recv.at[item],
            device_id={"rep": mate},
            device_id_type=MESH,
        )

    def peer_copy(item, step, group):
        return pltpu.make_async_remote_copy(
            src_ref=stage[item] if slim else original(item),
            dst_ref=crossing(item, group),
            send_sem=y_send.at[item, step - 1],
            recv_sem=y_recv.at[item, step - 1],
            device_id={"rep": peer(step)},
            device_id_type=MESH,
        )

    def forward_copy(item, step, group):
        return pltpu.make_async_remote_copy(
            src_ref=crossing(item, group),
            dst_ref=crossing(item, group),
            send_sem=f_send.at[item, step - 1],
            recv_sem=f_recv.at[item, step - 1],
            device_id={"rep": mate},
            device_id_type=MESH,
        )

    def near_here(item):
        local_copy(item).wait()
        mate_copy(item, mate).wait_recv()

    def start_out(item):
        if slim:
            near_here(item)
            for place in range(CAPACITY):
                stage[item][place] = buffers[item][send_sel[place]]
        for step in range(1, chips):
            peer_copy(item, step, rep).start()

    def start_near(item):
        mate_copy(item, rep).start()
        local_copy(item).start()

    def pass_on(item):
        for step in range(1, chips):
            peer_copy(item, step, source(step)).wait_recv()
            forward_copy(item, step, source(step)).start()

    def all_here(item):
        if not slim:
            near_here(item)
        for step in range(1, chips):
            forward_copy(item, step, mate_source(step)).wait_recv()

    def pick(item, slot):
        piece = buffers[item][sel[slot]]
        if slim:
            piece = jnp.where(from_far[slot] == 1, far[item][far_sel[slot]], piece)
        return piece

    def halo_copy(which, distance, part):
        placed = (kp, vp)[which]
        heads = pl.ds(part * PART_HEADS, PART_HEADS)
        return pltpu.make_async_remote_copy(
            src_ref=placed.at[heads, pl.ds(own_first, BLOCK), :],
            dst_ref=placed.at[heads, pl.ds((halo - distance) * BLOCK, BLOCK), :],
            send_sem=halo_send.at[which, distance - 1, part],
            recv_sem=halo_recv.at[which, distance - 1, part],
            device_id={"sp": lax.rem(shard + distance, shard_count)},
            device_id_type=MESH,
        )

    barrier = pltpu.get_barrier_semaphore()
    pl.semaphore_signal(barrier, inc=1, device_id={"rep": mate}, device_id_type=MESH)
    for step in range(1, chips):
        pl.semaphore_signal(barrier, inc=1, device_id={"rep": peer(step)}, device_id_type=MESH)
    for distance in range(1, halo + 1):

        @pl.when(shard + distance < shard_count)
        def _():
            pl.semaphore_signal(
                barrier, inc=1, device_id={"sp": shard + distance}, device_id_type=MESH
            )

        @pl.when(shard >= distance)
        def _():
            pl.semaphore_signal(
                barrier, inc=1, device_id={"sp": shard - distance}, device_id_type=MESH
            )

    before = jnp.minimum(shard, halo)
    after = jnp.minimum(shard_count - 1 - shard, halo)
    pl.semaphore_wait(barrier, chips + before + after)

    if slim:
        for item in range(2):
            start_near(item)
    else:
        for item in range(2):
            start_out(item)
        for item in range(2):
            start_near(item)
        for item in range(2, 2 + DEPTH):
            start_out(item)
            start_near(item)

    def table_at(of_chip, number):
        group = of_chip * 2 + number // DEVICE_PIECES
        return group, shard * DEVICE_PIECES + number % DEVICE_PIECES

    def find_slot(slot, carry):
        found = jnp.int32(0)
        for number in range((2 if slim else groups) * DEVICE_PIECES):
            at = table_at(chip if slim else 0, number)
            hit = (group_ref[at] == rep) & (slot_ref[at] == slot)
            found = jnp.where(hit, number, found)
        sel[slot] = found
        if slim:
            far_found, is_far, rank = jnp.int32(0), jnp.int32(0), jnp.int32(0)
            for number in range(2 * DEVICE_PIECES):
                at = table_at(1 - chip, number)
                group = group_ref[at]
                hit = (group == rep) & (slot_ref[at] == slot)
                far_found = jnp.where(hit, rank, far_found)
                is_far = jnp.where(hit, 1, is_far)
                rank = rank + jnp.where((group >= 2) == (chip == 1), 1, 0)
            far_sel[slot] = jnp.minimum(far_found, 2 * CAPACITY - 1)
            from_far[slot] = is_far
        return carry

    def find_sent(place, carry):
        found, rank = jnp.int32(0), jnp.int32(0)
        for number in range(2 * DEVICE_PIECES):
            leaves = (group_ref[table_at(chip, number)] >= 2) == (chip == 0)
            found = jnp.where(leaves & (rank == core * CAPACITY + place), number, found)
            rank = rank + jnp.where(leaves, 1, 0)
        send_sel[place] = found
        return carry

    if slim:
        lax.fori_loop(0, CAPACITY, find_sent, 0)
        for item in range(2):
            start_out(item)
        for item in range(2, 3 + DEPTH):
            start_near(item)
        for item in range(2, 2 + DEPTH):
            start_out(item)
    lax.fori_loop(0, DEVICE_PIECES, find_slot, 0)

    def first_token(positions):
        end = jnp.int32(0)
        first = jnp.zeros_like(positions)
        for document in range(lengths_ref.shape[1]):
            length = lengths_ref[0, document]
            end = end + length
            first = first + jnp.where(positions >= end, length, 0)
        return first

    for half in range(2):
        key_begin = (shard - halo) * BLOCK + half * HALF_ROWS
        key_positions = key_begin + lax.broadcasted_iota(jnp.int32, (1, window), 1)
        key_first = jnp.where(key_positions >= 0, first_token(key_positions), -1)
        query_begin = shard * BLOCK + half * HALF_ROWS
        query_positions = query_begin + lax.broadcasted_iota(jnp.int32, (HALF_ROWS, 1), 0)
        query_first = first_token(query_positions)
        allowed = (query_first == key_first) & (query_positions >= key_positions)
        bias[pl.ds(half * HALF_ROWS, HALF_ROWS), :] = jnp.where(allowed, 0.0, MASKED)

    for distance in range(1, halo + 1):

        @pl.when(shard < distance)
        def _():
            empty = jnp.zeros((KEY_VALUE_HEADS, BLOCK, HEAD_WIDTH), jnp.bfloat16)
            kp[:, pl.ds((halo - distance) * BLOCK, BLOCK), :] = empty
            vp[:, pl.ds((halo - distance) * BLOCK, BLOCK), :] = empty

    for item in range(2):
        pass_on(item)
    for item in range(2):
        all_here(item)
        placed = (kp, vp)[item]
        for slot in range(DEVICE_PIECES):
            piece = pick(item, slot)
            for head in range(KEY_VALUE_HEADS):
                placed[head, pl.ds(own_first + slot * PIECE_LENGTH, PIECE_LENGTH), :] = piece[
                    :, head * HEAD_WIDTH : (head + 1) * HEAD_WIDTH
                ]
    for part in range(PARTS):
        for distance in range(1, halo + 1):

            @pl.when(shard + distance < shard_count)
            def _():
                for which in range(2):
                    halo_copy(which, distance, part).start()

    factor = math.log2(math.e) / math.sqrt(HEAD_WIDTH)

    def out_copy(head):
        return pltpu.make_async_copy(
            obuf.at[lax.rem(head, 2)],
            o_hbm.at[:, pl.ds(pl.multiple_of(head * CHUNK, CHUNK), CHUNK)],
            out_sem.at[lax.rem(head, 2)],
        )

    def attend(head):
        buffer = lax.rem(head, 2)

        def one_piece(slot, carry):
            half = lax.div(slot, HALF_PIECES)
            keys_at = pl.ds(pl.multiple_of(half * HALF_ROWS, HALF_ROWS), window)
            rows_at = pl.ds(pl.multiple_of(slot * PIECE_LENGTH, PIECE_LENGTH), PIECE_LENGTH)
            piece = qsel[slot]
            query = jnp.concatenate(
                [piece[:, i * HEAD_WIDTH : (i + 1) * HEAD_WIDTH] for i in range(HEADS_PER_KV)],
                axis=0,
            )
            scores = lax.dot_general(
                query,
                kp[head, keys_at, :],
                (((1,), (1,)), ((), ())),
                preferred_element_type=jnp.float32,
            )
            scores = scores.reshape(HEADS_PER_KV, PIECE_LENGTH, window) * factor
            scores = (scores + bias[rows_at, :][None]).reshape(BLOCK, window)
            peak = jnp.max(scores, axis=1, keepdims=True)
            exponent = jnp.exp2(scores - peak)
            total = jnp.sum(exponent, axis=1, keepdims=True)
            summed = jnp.dot(
                exponent.astype(jnp.bfloat16),
                vp[head, keys_at, :],
                preferred_element_type=jnp.float32,
            )
            result = (summed / total).astype(jnp.bfloat16)
            for i in range(HEADS_PER_KV):
                obuf[buffer, rows_at, i * HEAD_WIDTH : (i + 1) * HEAD_WIDTH] = result[
                    i * PIECE_LENGTH : (i + 1) * PIECE_LENGTH
                ]
            return carry

        lax.fori_loop(0, DEVICE_PIECES, one_piece, 0)

    def turn(count, carry):
        for chunk in range(CHUNKS):

            @pl.when(count == chunk)
            def _():
                pass_on(2 + chunk)
                if chunk + DEPTH < CHUNKS:
                    for step in range(1, chips):
                        peer_copy(2 + chunk, step, rep).wait_send()
                    start_out(2 + chunk + DEPTH)
                    ahead = chunk + DEPTH + (1 if slim else 0)
                    if ahead < CHUNKS:
                        start_near(2 + ahead)

        for part in range(PARTS):

            @pl.when(count == 1 + part * PART_HEADS)
            def _():
                for distance in range(1, halo + 1):

                    @pl.when(shard >= distance)
                    def _():
                        for which in range(2):
                            halo_copy(which, distance, part).wait_recv()

        for chunk in range(CHUNKS):

            @pl.when(count == chunk + 1)
            def _():
                all_here(2 + chunk)
                for slot in range(DEVICE_PIECES):
                    qsel[slot] = pick(2 + chunk, slot)

        @pl.when(count >= 1)
        def _():
            head = count - 1

            @pl.when(count >= 3)
            def _():
                out_copy(head - 2).wait()

            attend(head)
            out_copy(head).start()

        return carry

    lax.fori_loop(0, CHUNKS + 1, turn, 0)

    for head in range(CHUNKS - 2, CHUNKS):
        out_copy(head).wait()
    for item in range(items):
        mate_copy(item, rep).wait_send()
        for step in range(1, chips):
            if item < 2 or item - 2 + DEPTH >= CHUNKS:
                peer_copy(item, step, rep).wait_send()
            forward_copy(item, step, source(step)).wait_send()
    for distance in range(1, halo + 1):

        @pl.when(shard + distance < shard_count)
        def _():
            for which in range(2):
                for part in range(PARTS):
                    halo_copy(which, distance, part).wait_send()


def gathered_attention(slim, groups, shard_count, operands):
    queries, keys, values, doc_lengths, dest_group, dest_slot = operands
    chips = groups // 2
    halo = shard_count // 4
    pieces = (2 if slim else groups) * DEVICE_PIECES
    items = CHUNKS + 2
    key_rows = (halo + 1) * BLOCK
    window = halo * BLOCK + HALF_ROWS
    wide = KEY_VALUE_HEADS * HEAD_WIDTH
    smem = pl.BlockSpec(memory_space=pltpu.SMEM)
    hbm = pl.BlockSpec(memory_space=pl.ANY)
    dma = pltpu.SemaphoreType.DMA
    widths = [wide] * 2 + [CHUNK] * CHUNKS
    scratch = []
    for count in (pieces, 2 * CAPACITY, CAPACITY) if slim else (pieces,):
        scratch += [pltpu.VMEM((count, PIECE_LENGTH, width), jnp.bfloat16) for width in widths]
    scratch += [
        pltpu.VMEM((KEY_VALUE_HEADS, key_rows, HEAD_WIDTH), jnp.bfloat16),
        pltpu.VMEM((KEY_VALUE_HEADS, key_rows, HEAD_WIDTH), jnp.bfloat16),
        pltpu.VMEM((BLOCK, window), jnp.float32),
        pltpu.VMEM((DEVICE_PIECES, PIECE_LENGTH, CHUNK), jnp.bfloat16),
        pltpu.VMEM((2, BLOCK, CHUNK), jnp.bfloat16),
        pltpu.SMEM((DEVICE_PIECES,), jnp.int32),
        pltpu.SMEM((DEVICE_PIECES,), jnp.int32),
        pltpu.SMEM((DEVICE_PIECES,), jnp.int32),
        pltpu.SMEM((CAPACITY,), jnp.int32),
        dma((items,)),
        dma((items, chips - 1)),
        dma((items, chips - 1)),
        dma((items,)),
        dma((items,)),
        dma((items, chips - 1)),
        dma((items, chips - 1)),
        dma((2, halo, PARTS)),
        dma((2, halo, PARTS)),
        dma((2,)),
    ]
    work = QUERY_HEADS * BLOCK * window
    return pl.pallas_call(
        functools.partial(kernel, groups, shard_count, halo, slim),
        out_shape=jax.ShapeDtypeStruct(queries.shape, jnp.bfloat16),
        in_specs=[smem, smem, smem, hbm, hbm, hbm],
        out_specs=hbm,
        scratch_shapes=scratch,
        cost_estimate=pl.CostEstimate(
            flops=4 * work * HEAD_WIDTH,
            bytes_accessed=4 * queries.size + 4 * keys.size,
            transcendentals=work,
        ),
        compiler_params=pltpu.CompilerParams(
            collective_id=1 if slim else 0, has_side_effects=True, vmem_limit_bytes=56 * 1024 * 1024
        ),
    )(
        doc_lengths,
        dest_group,
        dest_slot,
        queries.reshape(DEVICE_PIECES, PIECE_LENGTH, QUERY_HEADS * HEAD_WIDTH),
        keys.reshape(DEVICE_PIECES, PIECE_LENGTH, wide),
        values.reshape(DEVICE_PIECES, PIECE_LENGTH, wide),
    )


def shards(*operands):
    groups = lax.axis_size("rep")
    shard_count = lax.axis_size("sp")
    whole = functools.partial(gathered_attention, False, groups, shard_count)
    if groups != 4:
        return whole(operands)
    target_chip = operands[4].reshape(2, 2, shard_count, DEVICE_PIECES) // 2
    leaves = target_chip != jnp.arange(2)[:, None, None, None]
    fits = jnp.all(jnp.sum(leaves, axis=(1, 3)) <= 2 * CAPACITY)
    slim = functools.partial(gathered_attention, True, groups, shard_count)
    return lax.cond(fits, slim, whole, operands)


def solution(mesh):
    return jax.shard_map(
        shards,
        mesh=mesh,
        in_specs=(
            P(("rep", "sp"), None),
            P(("rep", "sp"), None),
            P(("rep", "sp"), None),
            P("rep", None),
            P(),
            P(),
        ),
        out_specs=P(("rep", "sp"), None),
        check_vma=False,
    )
```
